32 devices in a mesh: section: 2 (over core), dp: 4 (over z), tensor: 4 (over y, x).
Axes of the slice: x: 2, y: 2, z: 4, core: 2. Of those that a mesh axis runs over, the one named last changes fastest.
Arguments:
- inputs: bfloat16 [4, 4, 1024, 640], P(None, 'dp', 'tensor'), may hold values from -6 to 6
- cotangent: bfloat16 [4, 4, 1024, 640], P(None, 'dp', 'tensor'), may hold values from -6 to 6
- pre_attn_gain: bfloat16 [2, 640], P('section', 'dp'), may hold values from 0.25 to 1.75
- post_attn_gain: bfloat16 [2, 640], P('section', 'dp'), may hold values from 0.25 to 1.75
- pre_ffn_gain: bfloat16 [2, 640], P('section', 'dp'), may hold values from 0.25 to 1.75
- post_ffn_gain: bfloat16 [2, 640], P('section', 'dp'), may hold values from 0.25 to 1.75
- query_gain: bfloat16 [2, 256], P('section', 'dp'), may hold values from 0.25 to 1.75
- key_gain: bfloat16 [2, 256], P('section', 'dp'), may hold values from 0.25 to 1.75
- query_weight: bfloat16 [2, 640, 1024], P('section', 'dp', 'tensor'), may hold values from -0.25 to 0.25
- key_weight: bfloat16 [2, 640, 256], P('section', 'dp'), may hold values from -0.25 to 0.25
- value_weight: bfloat16 [2, 640, 256], P('section', 'dp'), may hold values from -0.25 to 0.25
- out_weight: bfloat16 [2, 1024, 640], P('section', 'tensor', 'dp'), may hold values from -0.1875 to 0.1875
- gate_weight: bfloat16 [2, 640, 2048], P('section', 'dp', 'tensor'), may hold values from -0.25 to 0.25
- up_weight: bfloat16 [2, 640, 2048], P('section', 'dp', 'tensor'), may hold values from -0.25 to 0.25
- down_weight: bfloat16 [2, 2048, 640], P('section', 'tensor', 'dp'), may hold values from -0.125 to 0.125
Outputs:
- layer_outputs: bfloat16 [2, 4, 4, 1024, 640], P('section', None, 'dp', 'tensor')
- input_grads: float32 [2, 4, 4, 1024, 640], P('section', None, 'dp', 'tensor')
- grad_pre_attn_gain: float32 [2, 640], P('section', 'dp')
- grad_post_attn_gain: float32 [2, 640], P('section', 'dp')
- grad_pre_ffn_gain: float32 [2, 640], P('section', 'dp')
- grad_post_ffn_gain: float32 [2, 640], P('section', 'dp')
- grad_query_gain: float32 [2, 256], P('section', 'dp')
- grad_key_gain: float32 [2, 256], P('section', 'dp')
- grad_query_weight: float32 [2, 640, 1024], P('section', 'dp', 'tensor')
- grad_key_weight: float32 [2, 640, 256], P('section', 'dp')
- grad_value_weight: float32 [2, 640, 256], P('section', 'dp')
- grad_out_weight: float32 [2, 1024, 640], P('section', 'tensor', 'dp')
- grad_gate_weight: float32 [2, 640, 2048], P('section', 'dp', 'tensor')
- grad_up_weight: float32 [2, 640, 2048], P('section', 'dp', 'tensor')
- grad_down_weight: float32 [2, 2048, 640], P('section', 'tensor', 'dp')
The draws below stay inside these ranges and needn't reach their ends.
All inputs are finite; a program needn't handle non-finite values.
Results may differ from the reference program's by a relative error of at most 0.038.
Values may be sent and summed in bfloat16 or wider, within the bound.
A program may use at most 256 MiB of HBM per device.

```python
import math
import jax
import jax.numpy as jnp
from jax import lax

D = 640
NH = 4
HD = 256
FF = 2048
WIN = 512
SEQ_LEN = 1024
MB = 4
BATCH = 4
LAYERS = 2


def shard_levels(stream_key, extent, pieces, low, high):
    def one(axis_at, blocks):
        draws = jax.random.uniform(jax.random.fold_in(jax.random.fold_in(stream_key, 6), axis_at), (blocks,), jnp.float32, low / len(pieces), high / len(pieces))
        return jnp.repeat(jnp.exp(draws), extent[axis_at] // blocks).reshape((-1,) + (1,) * (len(extent) - axis_at - 1))

    factor_of = one(*pieces[0])
    for cut in pieces[1:]:
        factor_of = factor_of * one(*cut)
    return factor_of


def normal_values(key, shape, width, bound, cuts=(), kind=jnp.bfloat16):
    gain = shard_levels(key, shape, cuts, -0.22, 0.18) if cuts else 1.0
    values = jax.random.normal(key, shape, jnp.float32) * width * gain
    return jnp.minimum(jnp.maximum(values, -bound), bound).astype(kind)


def setup_inputs(seed: int = 0) -> dict:
    key_of = jax.random.split(jax.random.key(seed), 16)
    return {
        "inputs": normal_values(key_of[0], (MB, BATCH, SEQ_LEN, D), 1.0, 6.0, ((1, 4), (2, 4))),
        "cotangent": normal_values(key_of[1], (MB, BATCH, SEQ_LEN, D), 1.0, 6.0, ((1, 4), (2, 4))),
        "pre_attn_gain": jnp.clip(1.0 + 0.15 * jax.random.normal(key_of[2], (LAYERS, D), jnp.float32), 0.25, 1.75).astype(jnp.bfloat16),
        "post_attn_gain": jnp.clip(1.0 + 0.15 * jax.random.normal(key_of[3], (LAYERS, D), jnp.float32), 0.25, 1.75).astype(jnp.bfloat16),
        "pre_ffn_gain": jnp.clip(1.0 + 0.15 * jax.random.normal(key_of[4], (LAYERS, D), jnp.float32), 0.25, 1.75).astype(jnp.bfloat16),
        "post_ffn_gain": jnp.clip(1.0 + 0.15 * jax.random.normal(key_of[5], (LAYERS, D), jnp.float32), 0.25, 1.75).astype(jnp.bfloat16),
        "query_gain": jnp.clip(1.0 + 0.15 * jax.random.normal(key_of[6], (LAYERS, HD), jnp.float32), 0.25, 1.75).astype(jnp.bfloat16),
        "key_gain": jnp.clip(1.0 + 0.15 * jax.random.normal(key_of[7], (LAYERS, HD), jnp.float32), 0.25, 1.75).astype(jnp.bfloat16),
        "query_weight": normal_values(key_of[8], (LAYERS, D, NH * HD), D ** -0.5, 0.25, ((0, 2), (1, 4), (2, 4))),
        "key_weight": normal_values(key_of[9], (LAYERS, D, HD), D ** -0.5, 0.25, ((0, 2), (1, 4))),
        "value_weight": normal_values(key_of[10], (LAYERS, D, HD), D ** -0.5, 0.25, ((0, 2), (1, 4))),
        "out_weight": normal_values(key_of[11], (LAYERS, NH * HD, D), (NH * HD) ** -0.5, 0.1875, ((0, 2), (1, 4), (2, 4))),
        "gate_weight": normal_values(key_of[12], (LAYERS, D, FF), D ** -0.5, 0.25, ((0, 2), (1, 4), (2, 4))),
        "up_weight": normal_values(key_of[13], (LAYERS, D, FF), D ** -0.5, 0.25, ((0, 2), (1, 4), (2, 4))),
        "down_weight": normal_values(key_of[14], (LAYERS, FF, D), FF ** -0.5, 0.125, ((0, 2), (1, 4), (2, 4))),
    }


@jax.custom_vjp
def low(v):
    return lax.optimization_barrier(v.astype(jnp.bfloat16)).astype(jnp.float32)

@jax.custom_vjp
def low_back(v):
    return v

def low_keep(v):
    return (low(v), None)

def low_pass(kept, grad):
    return (grad,)

def back_keep(v):
    return (v, None)

def back_low(kept, grad):
    return (low(grad),)
low.defvjp(low_keep, low_pass)
low_back.defvjp(back_keep, back_low)
EPSILON = 1e-06
PRECISE = lax.Precision.HIGHEST
NEGATIVE = -1e+30

def norm_gain(values, scales):
    return values * lax.rsqrt(lax.optimization_barrier(jnp.mean(values * values, axis=-1, keepdims=True)) + EPSILON) * scales

def matmul(left_side, right_side):
    return jnp.dot(left_side, right_side, precision=PRECISE, preferred_element_type=jnp.float32)

def rotary_tables(length, dimension):
    halved = dimension // 2
    positions = jnp.arange(length, dtype=jnp.int32).astype(jnp.float32)
    indices = jnp.arange(halved, dtype=jnp.int32).astype(jnp.float32)
    inverse = jnp.exp(indices * (-2.0 * math.log(10000.0) / dimension))
    angles = positions[:, None] * inverse[None, :]
    return (jnp.cos(angles), jnp.sin(angles))

def rotate(values, cosine_table, sine_table):
    halved = values.shape[-1] // 2
    former = values[..., :halved]
    latter = values[..., halved:]
    return jnp.concatenate([former * cosine_table - latter * sine_table, latter * cosine_table + former * sine_table], axis=-1)

def layer(params, layer_index, inputs):
    pre_attn, post_attn, pre_ffn, post_ffn, query_scale, key_scale, projected_queries, projected_keys, projected_values, output_projected, gate_weight_matrix, up_weight_matrix, down_weight_matrix = [weight[layer_index] for weight in params]
    length = inputs.shape[0]
    cosine_table, sine_table = rotary_tables(length, HD)
    normalized_rows = low(norm_gain(inputs, pre_attn))
    query_raw = low_back(matmul(normalized_rows, projected_queries)).reshape(length, NH, HD)
    unrotated_keys = low_back(matmul(normalized_rows, projected_keys))
    values_all = low(low_back(matmul(normalized_rows, projected_values)))
    queries = low(rotate(norm_gain(query_raw, query_scale), cosine_table[:, None, :], sine_table[:, None, :]) * HD ** (-0.5))
    keys_all = low(rotate(norm_gain(unrotated_keys, key_scale), cosine_table, sine_table))
    block_rows = min(512, length)
    starts = jnp.arange(length // block_rows, dtype=jnp.int32) * block_rows
    grouped = queries.reshape(length // block_rows, block_rows, NH, HD)

    def attend(item_pair):
        query_block, offset = item_pair
        scores = low_back(jnp.einsum('qhd,kd->hqk', query_block, keys_all, precision=PRECISE))
        query_pos = offset + jnp.arange(block_rows, dtype=jnp.int32)
        key_pos = jnp.arange(length, dtype=jnp.int32)
        allowed = (key_pos[None, :] <= query_pos[:, None]) & (query_pos[:, None] - key_pos[None, :] < WIN)
        scores = jnp.where(allowed[None], scores, NEGATIVE)
        highest = lax.optimization_barrier(jnp.max(scores, axis=-1, keepdims=True))
        log_total = highest + jnp.log(lax.optimization_barrier(jnp.sum(jnp.exp(scores - highest), axis=-1, keepdims=True)))
        weights = low(jnp.exp(scores - log_total))
        return jnp.einsum('hqk,kd->qhd', weights, values_all, precision=PRECISE)
    attention_out = lax.map(jax.checkpoint(attend), (grouped, starts))
    attended_rows = low(low_back(attention_out.reshape(length, NH * HD)))
    branch = low_back(matmul(attended_rows, output_projected))
    hidden = inputs + norm_gain(branch, post_attn)
    feedforward_input = low(norm_gain(hidden, pre_ffn))
    gate_proj = low_back(matmul(feedforward_input, gate_weight_matrix))
    projected_up = low_back(matmul(feedforward_input, up_weight_matrix))
    gated_product = low(jax.nn.gelu(gate_proj, approximate=True) * projected_up)
    ffn_output = low_back(matmul(gated_product, down_weight_matrix))
    return hidden + norm_gain(ffn_output, post_ffn)

def two_layers(params, inputs, probe_zero):
    middle = low(low_back(layer(params, 0, inputs) + probe_zero))
    return (low(layer(params, 1, middle)), middle)

def reference(inputs, cotangent, pre_attn_gain, post_attn_gain, pre_ffn_gain, post_ffn_gain, query_gain, key_gain, query_weight, key_weight, value_weight, out_weight, gate_weight, up_weight, down_weight):
    params = tuple((weight.astype(jnp.float32) for weight in (pre_attn_gain, post_attn_gain, pre_ffn_gain, post_ffn_gain, query_gain, key_gain, query_weight, key_weight, value_weight, out_weight, gate_weight, up_weight, down_weight)))
    count_all = MB * BATCH
    shape_flat = (count_all, SEQ_LEN, D)
    flat_in = inputs.astype(jnp.float32).reshape(shape_flat)
    flat_cot = cotangent.astype(jnp.float32).reshape(shape_flat)

    def advance(running, item_pair):
        sequence, seq_cot = item_pair
        probe_zero = jnp.zeros_like(sequence)
        (final_out, middle), pullback = jax.vjp(two_layers, params, sequence, probe_zero)
        gradients, grad_in, grad_mid = pullback((seq_cot, jnp.zeros_like(middle)))
        running = tuple((summed + update for summed, update in zip(running, gradients)))
        return (running, (middle, final_out, grad_in, grad_mid))
    zero_grads = tuple((jnp.zeros_like(weight) for weight in params))
    totals, (middles, finals, grad_ins, grad_mids) = lax.scan(advance, zero_grads, (flat_in, flat_cot))
    full_shape = (MB, BATCH, SEQ_LEN, D)
    layer_outputs = jnp.stack([middles.reshape(full_shape), finals.reshape(full_shape)]).astype(jnp.bfloat16)
    input_grads = jnp.stack([grad_ins.reshape(full_shape), grad_mids.reshape(full_shape)])
    return (layer_outputs, input_grads, totals[0], totals[1], totals[2], totals[3], totals[4], totals[5], totals[6], totals[7], totals[8], totals[9], totals[10], totals[11], totals[12])
```

```python
from functools import partial
import math

import jax
import jax.numpy as jnp
from jax import lax
from jax.sharding import PartitionSpec as P

WIN = 512


EPSILON = 1e-06
NEGATIVE = -1e30


def norm_gain(values, scales):
    return values * lax.rsqrt(jnp.mean(values * values, axis=-1, keepdims=True) + EPSILON) * scales


def rotate(values, cosine_table, sine_table):
    halved = values.shape[-1] // 2
    former = values[..., :halved]
    latter = values[..., halved:]
    return jnp.concatenate(
        [former * cosine_table - latter * sine_table, latter * cosine_table + former * sine_table],
        axis=-1,
    )


def query_path(raw_values, scales, cosine_table, sine_table):
    return rotate(norm_gain(raw_values, scales), cosine_table, sine_table) * raw_values.shape[
        -1
    ] ** (-0.5)


def key_path(raw_values, scales, cosine_table, sine_table):
    return rotate(norm_gain(raw_values, scales), cosine_table, sine_table)


def gated_unit(gate_proj, projected_up):
    return jax.nn.gelu(gate_proj, approximate=True) * projected_up


def cross(block):
    return lax.ppermute(block, "section", [(0, 1), (1, 0)])


def half_swap(mine, pair_rows):
    core = lax.axis_index("section")
    keep = lax.dynamic_slice_in_dim(mine, core * pair_rows, pair_rows, axis=0)
    give = lax.dynamic_slice_in_dim(mine, (1 - core) * pair_rows, pair_rows, axis=0)
    got = cross(give)
    first = core == 0
    return jnp.where(first, keep, got), jnp.where(first, got, keep)


def gather_all(shard):
    return lax.all_gather(shard, ("tensor", "dp", "section"), axis=0, tiled=True)


def dot(spec, left, right):
    return jnp.einsum(spec, left, right, preferred_element_type=jnp.float32)


def score_parts(tensor_size, span):
    half = span // 2
    reach = -(-WIN // span)
    parts = []
    step = max(1, min(tensor_size, reach))
    for begin in range(0, tensor_size, step):
        end = min(begin + step, tensor_size)
        parts.append((begin * half, end * half, max(0, begin - reach) * span, end * span))
    return parts


def masked_scores(queries, keys, row_pos, part):
    r0, r1, k0, k1 = part
    scores = dot("hqd,kd->hqk", queries[:, r0:r1], keys[k0:k1])
    distance = row_pos[r0:r1, None] - jnp.arange(k0, k1, dtype=jnp.int32)[None, :]
    return jnp.where((distance >= 0) & (distance < WIN), scores, NEGATIVE)


def natural_order(mine, tensor_size):
    other = cross(mine)
    first = lax.axis_index("section") == 0
    width = mine.shape[-1]
    pair = jnp.stack(
        [
            jnp.where(first, mine, other).reshape(tensor_size, -1, width),
            jnp.where(first, other, mine).reshape(tensor_size, -1, width),
        ],
        axis=1,
    )
    return pair.reshape(-1, width)


def sum_own(whole, tensor_size):
    core = lax.axis_index("section")
    width = whole.shape[-1]
    split = whole.reshape(tensor_size, 2, -1, width)
    own = lax.dynamic_index_in_dim(split, core, axis=1, keepdims=False)
    give = lax.dynamic_index_in_dim(split, 1 - core, axis=1, keepdims=False)
    got = cross(give.astype(jnp.bfloat16)).astype(jnp.float32)
    return (own + got).reshape(-1, width)


def forward_attention(u, weights, gains, row_pos, tables, tensor_size, span):
    pre_attn, post_attn, pre_ffn, post_ffn, query_scale, key_scale = gains
    wq, wo, wkv = weights
    cos_rows, sin_rows = tables
    head = wq.shape[2]
    normed = norm_gain(u, pre_attn).astype(jnp.bfloat16)
    kv_raw = dot("mv,vn->mn", normed, wkv)
    key_raw, values = kv_raw[:, :head], kv_raw[:, head:].astype(jnp.bfloat16)
    keys = key_path(key_raw, key_scale, cos_rows, sin_rows).astype(jnp.bfloat16)
    kv_all = natural_order(jnp.concatenate([keys, values], axis=-1), tensor_size)
    keys_all, values_all = kv_all[:, :head], kv_all[:, head:]
    query_raw = dot("mv,tvn->tmn", normed, wq)
    queries = query_path(query_raw, query_scale, cos_rows, sin_rows).astype(jnp.bfloat16)
    outs, totals = [], []
    for part in score_parts(tensor_size, span):
        scores = masked_scores(queries, keys_all, row_pos, part)
        highest = jnp.max(scores, axis=-1, keepdims=True)
        log_total = highest + jnp.log(jnp.sum(jnp.exp(scores - highest), axis=-1, keepdims=True))
        probs = jnp.exp(scores - log_total).astype(jnp.bfloat16)
        outs.append(dot("hqk,kd->hqd", probs, values_all[part[2] : part[3]]).astype(jnp.bfloat16))
        totals.append(log_total)
    attended = jnp.concatenate(outs, axis=1)
    branch = dot("tmn,tvn->mv", attended, wo)
    hidden = u + norm_gain(branch, post_attn)
    kept = (u, normed, query_raw, key_raw, queries, keys_all, values_all, totals, attended, branch)
    return hidden, kept


def forward_ffn(hidden, weights, gains):
    pre_ffn, post_ffn = gains[2], gains[3]
    wg, wu, wd = weights
    ffn_input = norm_gain(hidden, pre_ffn).astype(jnp.bfloat16)
    gate_proj = dot("mv,tvn->tmn", ffn_input, wg)
    up_proj = dot("mv,tvn->tmn", ffn_input, wu)
    product = gated_unit(gate_proj, up_proj).astype(jnp.bfloat16)
    ffn_output = dot("tmn,tvn->mv", product, wd)
    result = hidden + norm_gain(ffn_output, post_ffn)
    return result, (hidden, ffn_input, gate_proj, up_proj, product, ffn_output)


def backward_ffn(grad_output, kept, weights, gains):
    pre_ffn, post_ffn = gains[2], gains[3]
    wg, wu, wd = weights
    hidden, ffn_input, gate_proj, up_proj, product, ffn_output = kept
    output_grad, post_ffn_grad = jax.vjp(norm_gain, ffn_output, post_ffn)[1](grad_output)
    output_grad = output_grad.astype(jnp.bfloat16)
    product_grad = dot("mv,tvn->tmn", output_grad, wd)
    down_grad = dot("mv,tmn->tvn", output_grad, product).astype(jnp.bfloat16)
    gate_grad, up_grad = jax.vjp(gated_unit, gate_proj, up_proj)[1](product_grad)
    gate_grad = gate_grad.astype(jnp.bfloat16)
    up_grad = up_grad.astype(jnp.bfloat16)
    ffn_input_grad = dot("tmn,tvn->mv", gate_grad, wg) + dot("tmn,tvn->mv", up_grad, wu)
    gate_weight_grad = dot("mv,tmn->tvn", ffn_input, gate_grad).astype(jnp.bfloat16)
    up_weight_grad = dot("mv,tmn->tvn", ffn_input, up_grad).astype(jnp.bfloat16)
    hidden_part, pre_ffn_grad = jax.vjp(norm_gain, hidden, pre_ffn)[1](ffn_input_grad)
    hidden_grad = grad_output + hidden_part
    packed = jnp.concatenate([gate_weight_grad, up_weight_grad, down_grad], axis=-1)
    return hidden_grad, packed, (pre_ffn_grad, post_ffn_grad)


def backward_attention(hidden_grad, kept, weights, gains, row_pos, tables, tensor_size, span):
    pre_attn, post_attn, pre_ffn, post_ffn, query_scale, key_scale = gains
    wq, wo, wkv = weights
    cos_rows, sin_rows = tables
    u, normed, query_raw, key_raw, queries, keys_all, values_all, totals, attended, branch = kept
    head = wq.shape[2]
    length = keys_all.shape[0]
    branch_grad, post_attn_grad = jax.vjp(norm_gain, branch, post_attn)[1](hidden_grad)
    branch_grad = branch_grad.astype(jnp.bfloat16)
    attended_grad = dot("mv,tvn->tmn", branch_grad, wo).astype(jnp.bfloat16)
    out_grad = dot("mv,tmn->tvn", branch_grad, attended).astype(jnp.bfloat16)
    query_grads = []
    kv_sum = jnp.zeros((length, 2 * head), jnp.float32)
    for part, log_total in zip(score_parts(tensor_size, span), totals):
        r0, r1, k0, k1 = part
        weights_exact = jnp.exp(masked_scores(queries, keys_all, row_pos, part) - log_total)
        out_block = attended_grad[:, r0:r1]
        probs_grad = dot("hqd,kd->hqk", out_block, values_all[k0:k1])
        inner = jnp.sum(weights_exact * probs_grad, axis=-1, keepdims=True)
        score_grad = (weights_exact * (probs_grad - inner)).astype(jnp.bfloat16)
        query_grads.append(dot("hqk,kd->hqd", score_grad, keys_all[k0:k1]))
        key_term = dot("hqk,hqd->kd", score_grad, queries[:, r0:r1])
        value_term = dot("hqk,hqd->kd", weights_exact.astype(jnp.bfloat16), out_block)
        kv_term = jnp.concatenate([key_term, value_term], axis=-1)
        kv_sum = kv_sum + jnp.pad(kv_term, ((k0, length - k1), (0, 0)))
    kv_own = sum_own(kv_sum, tensor_size)
    query_grad = jnp.concatenate(query_grads, axis=1)
    value_grad = kv_own[:, head:].astype(jnp.bfloat16)
    raw_query_grad, query_scale_grad = jax.vjp(
        partial(query_path, cosine_table=cos_rows, sine_table=sin_rows), query_raw, query_scale
    )[1](query_grad)
    raw_query_grad = raw_query_grad.astype(jnp.bfloat16)
    raw_key_grad, key_scale_grad = jax.vjp(
        partial(key_path, cosine_table=cos_rows, sine_table=sin_rows), key_raw, key_scale
    )[1](kv_own[:, :head])
    raw_kv_grad = jnp.concatenate([raw_key_grad.astype(jnp.bfloat16), value_grad], axis=-1)
    normed_grad = dot("tmn,tvn->mv", raw_query_grad, wq) + dot("mn,vn->mv", raw_kv_grad, wkv)
    query_weight_grad = dot("mv,tmn->tvn", normed, raw_query_grad).astype(jnp.bfloat16)
    kv_weight_grad = dot("mv,mn->vn", normed, raw_kv_grad).astype(jnp.bfloat16)
    input_part, pre_attn_grad = jax.vjp(norm_gain, u, pre_attn)[1](normed_grad)
    u_grad = hidden_grad + input_part
    return (
        u_grad,
        (query_weight_grad, out_grad, kv_weight_grad),
        (pre_attn_grad, post_attn_grad, query_scale_grad, key_scale_grad),
    )


def reduce_packed(packed, rows):
    tensor_size, _, width = packed.shape
    core = lax.axis_index("section")
    split = packed.reshape(tensor_size, -1, 2, rows // 2, width)
    own = lax.dynamic_index_in_dim(split, core, axis=2, keepdims=False)
    give = lax.dynamic_index_in_dim(split, 1 - core, axis=2, keepdims=False)
    total = own.astype(jnp.float32) + cross(give).astype(jnp.float32)
    total = total.astype(jnp.bfloat16).reshape(-1, width)
    total = lax.psum_scatter(total, "tensor", scatter_dimension=0, tiled=True)
    return lax.psum_scatter(total, "dp", scatter_dimension=0, tiled=True)


def own_layer(halves):
    first = lax.axis_index("section") == 0
    keep = jnp.where(first, halves[0], halves[1])
    got = cross(jnp.where(first, halves[1], halves[0]))
    return jnp.concatenate(
        [jnp.where(first, keep, got), jnp.where(first, got, keep)], axis=0
    ).astype(jnp.float32)


def local(
    inputs,
    cotangent,
    pre_attn_gain,
    post_attn_gain,
    pre_ffn_gain,
    post_ffn_gain,
    query_gain,
    key_gain,
    query_weight,
    key_weight,
    value_weight,
    out_weight,
    gate_weight,
    up_weight,
    down_weight,
):
    tensor_size = lax.axis_size("tensor")
    dp_size = lax.axis_size("dp")
    core = lax.axis_index("section")
    micro_count, _, span, width = inputs.shape
    half = span // 2
    rows, head = query_weight.shape[1:]
    hidden_cols = gate_weight.shape[2]
    depth = rows * dp_size

    def to_chip(block):
        own = lax.dynamic_slice_in_dim(block[:, 0], core * half, half, axis=1)
        moved = lax.all_to_all(own, "tensor", split_axis=0, concat_axis=0, tiled=True)
        return moved.reshape(-1, width)

    def from_chip(first_layer, second_layer):
        both = jnp.stack([first_layer, second_layer]).reshape(2 * tensor_size, half, width)
        moved = lax.all_to_all(both, ("section", "tensor"), split_axis=0, concat_axis=0, tiled=True)
        moved = moved.reshape(2, tensor_size, half, width).transpose(1, 0, 2, 3)
        return moved.reshape(1, tensor_size, 1, span, width)

    gain_parts = (pre_attn_gain, post_attn_gain, pre_ffn_gain, post_ffn_gain, query_gain, key_gain)
    gain_sizes = [part.shape[1] for part in gain_parts]
    gain_row = jnp.concatenate([part[0] for part in gain_parts])
    gain_all = lax.all_gather(gain_row, ("section", "dp"), axis=0, tiled=True)
    gain_all = gain_all.reshape(2, dp_size, -1).astype(jnp.float32)
    gains = []
    for index in range(2):
        pieces, at = [], 0
        for size in gain_sizes:
            pieces.append(gain_all[index, :, at : at + size].reshape(-1))
            at += size
        gains.append(tuple(pieces))

    quarter = rows // tensor_size
    kv_rows = jnp.concatenate([key_weight[0], value_weight[0]], axis=-1)
    kv_rows = lax.dynamic_slice_in_dim(
        kv_rows, lax.axis_index("tensor") * quarter, quarter, axis=0
    ).reshape(rows, -1)
    attention_shard = jnp.concatenate([query_weight[0], out_weight[0].T, kv_rows], axis=-1)
    ffn_shard = jnp.concatenate([gate_weight[0], up_weight[0], down_weight[0].T], axis=-1)
    attention_shards = half_swap(attention_shard, rows // 2)
    ffn_shards = half_swap(ffn_shard, rows // 2)

    def attention_weights(index):
        whole = gather_all(attention_shards[index]).reshape(tensor_size, depth, -1)
        wkv = whole[:, :, 2 * head :].reshape(tensor_size, dp_size, quarter, 2 * head)
        wkv = wkv.transpose(1, 0, 2, 3).reshape(depth, 2 * head)
        return whole[:, :, :head], whole[:, :, head : 2 * head], wkv

    def ffn_weights(index):
        whole = gather_all(ffn_shards[index]).reshape(tensor_size, depth, -1)
        return tuple(
            whole[:, :, n * hidden_cols : (n + 1) * hidden_cols] for n in range(3)
        )

    stream = to_chip(inputs).astype(jnp.float32)
    attention = [attention_weights(0), None]
    ffn = [ffn_weights(0), None]
    attention[1] = attention_weights(1)
    ffn[1] = ffn_weights(1)
    length = span * tensor_size
    row = jnp.arange(tensor_size * half, dtype=jnp.int32)
    row_pos = (row // half) * span + core * half + row % half
    halved = head // 2
    indices = jnp.arange(halved, dtype=jnp.int32).astype(jnp.float32)
    inverse = jnp.exp(indices * (-2.0 * math.log(10000.0) / head))
    angles = row_pos.astype(jnp.float32)[:, None] * inverse[None, :]
    tables = (jnp.cos(angles), jnp.sin(angles))

    kept_attention, kept_ffn, rounded = [], [], []
    for index in range(2):
        hidden, kept = forward_attention(
            stream, attention[index], gains[index], row_pos, tables, tensor_size, span
        )
        kept_attention.append(kept)
        result, kept = forward_ffn(hidden, ffn[index], gains[index])
        kept_ffn.append(kept)
        rounded.append(result.astype(jnp.bfloat16))
        stream = rounded[-1].astype(jnp.float32)
    layer_outputs = from_chip(rounded[0], rounded[1])

    grad = to_chip(cotangent).astype(jnp.float32)
    attention_sums, ffn_sums, input_grads = [None, None], [None, None], [None, None]
    for index in (1, 0):
        grad, packed, ffn_gain_grads = backward_ffn(
            grad, kept_ffn[index], ffn[index], gains[index]
        )
        ffn_sums[index] = reduce_packed(packed, rows)
        grad, matrix_grads, gain_grads = backward_attention(
            grad,
            kept_attention[index],
            attention[index],
            gains[index],
            row_pos,
            tables,
            tensor_size,
            span,
        )
        gain_list = gain_grads[:2] + ffn_gain_grads + gain_grads[2:]
        gain_block = jnp.concatenate([part.reshape(dp_size, -1) for part in gain_list], axis=1)
        count = gain_block.shape[1]
        lanes = max(128, -(-count // rows))
        gain_block = jnp.pad(gain_block, ((0, 0), (0, rows * lanes - count)))
        gain_block = gain_block.reshape(depth, lanes).astype(jnp.bfloat16)
        shared = jnp.concatenate([matrix_grads[2], gain_block], axis=-1)
        shared = jnp.broadcast_to(shared[None], (tensor_size,) + shared.shape)
        packed = jnp.concatenate([matrix_grads[0], matrix_grads[1], shared], axis=-1)
        attention_sums[index] = reduce_packed(packed, rows)
        rounded_grad = grad.astype(jnp.bfloat16)
        input_grads[index] = rounded_grad
        grad = rounded_grad.astype(jnp.float32)

    input_grad = from_chip(input_grads[0], input_grads[1]).astype(jnp.float32)
    ffn_total = own_layer(ffn_sums)
    attention_total = own_layer(attention_sums)
    gain_total = attention_total[:, 4 * head :].reshape(-1)
    gain_outs, at = [], 0
    for size in gain_sizes:
        gain_outs.append(gain_total[at : at + size])
        at += size
    finished = tuple(gain_outs) + (
        attention_total[:, :head],
        attention_total[:, 2 * head : 3 * head],
        attention_total[:, 3 * head : 4 * head],
        attention_total[:, head : 2 * head].T,
        ffn_total[:, :hidden_cols],
        ffn_total[:, hidden_cols : 2 * hidden_cols],
        ffn_total[:, 2 * hidden_cols :].T,
    )
    return (layer_outputs, input_grad) + tuple(part[None] for part in finished)


def solution(mesh):
    return jax.shard_map(
        local,
        mesh=mesh,
        in_specs=(
            P(None, "dp", "tensor", None),
            P(None, "dp", "tensor", None),
            P("section", "dp"),
            P("section", "dp"),
            P("section", "dp"),
            P("section", "dp"),
            P("section", "dp"),
            P("section", "dp"),
            P("section", "dp", "tensor"),
            P("section", "dp", None),
            P("section", "dp", None),
            P("section", "tensor", "dp"),
            P("section", "dp", "tensor"),
            P("section", "dp", "tensor"),
            P("section", "tensor", "dp"),
        ),
        out_specs=(
            P("section", None, "dp", "tensor", None),
            P("section", None, "dp", "tensor", None),
            P("section", "dp"),
            P("section", "dp"),
            P("section", "dp"),
            P("section", "dp"),
            P("section", "dp"),
            P("section", "dp"),
            P("section", "dp", "tensor"),
            P("section", "dp", None),
            P("section", "dp", None),
            P("section", "tensor", "dp"),
            P("section", "dp", "tensor"),
            P("section", "dp", "tensor"),
            P("section", "tensor", "dp"),
        ),
        check_vma=False,
    )
```
